32 devices in a mesh: row: 8 (over z, y), col: 4 (over x, core).
Axes of the slice: x: 2, y: 2, z: 4, core: 2. Of those that a mesh axis runs over, the one named last changes fastest.
Arguments:
- density: float32 [8, 8, 4, 128, 128], P('row', 'col'), as said below
- pattern: int32 [8, 8, 4], P('row', 'col'), may hold values from 0 to 8, as said below
- retained: int32 [8, 8, 4], P('row', 'col'), may hold values from 0 to 8, as said below
Outputs:
- purified: float32 [8, 8, 4, 128, 128], P('row', 'col')
The draws below stay inside these ranges and needn't reach their ends.
Inputs may be any that keep to these rules, and one draw needn't show every extreme that they name: Slot 0 of every block row holds code 4, the site itself; the 4 codes of a block row are distinct; the pattern is symmetric: x holds c exactly when x + offset(c) holds 8 - c. `retained`: slot 0 of every block row holds code 4, the site itself; the 4 codes of a block row are distinct; the pattern is symmetric: x holds c exactly when x + offset(c) holds 8 - c. `density`: the matrix is symmetric: the block of x on code c is the transpose of the block of x + offset(c) on code 8 - c, and every block on code 4 is symmetric.
All inputs are finite; a program needn't handle non-finite values.
Results may differ from the reference program's by a relative error of at most 0.0003.
Values sent between devices are 32-bit elements; how exact they have to be, the bound alone decides.
A program may use at most 64 MiB of HBM per device.

```python
import jax
import jax.numpy as jnp
from jax import lax

BLOCK = 128
SLOTS = 4
STEPS = 2
SITES_A = 8
SITES_B = 8


def draw_codes(key):
    axis_key = jax.random.fold_in(key, 1)
    parity_a_key = jax.random.fold_in(key, 3)
    parity_b_key = jax.random.fold_in(key, 4)
    order_key = jax.random.fold_in(key, 5)
    matched_axis = jax.random.randint(axis_key, (), 0, 2, dtype=jnp.int32)
    parity_cols = jax.random.randint(parity_a_key, (SITES_B,), 0, 2, dtype=jnp.int32)
    parity_rows = jax.random.randint(parity_b_key, (SITES_A,), 0, 2, dtype=jnp.int32)
    grid_a = jnp.arange(SITES_A, dtype=jnp.int32)[:, None]
    grid_b = jnp.arange(SITES_B, dtype=jnp.int32)[None, :]
    match_first = jnp.where((grid_a + parity_cols[None, :]) % 2 == 0, 7, 1)
    match_second = jnp.where((grid_b + parity_rows[:, None]) % 2 == 0, 5, 3)
    matched = jnp.where(matched_axis == 0, match_first, match_second).astype(jnp.int32)
    lower = jnp.zeros((SITES_A, SITES_B), jnp.int32)
    upper = (8 - lower).astype(jnp.int32)
    three = jnp.stack([lower, upper, matched], axis=2)
    shuffled = jax.random.permutation(order_key, three, axis=2, independent=True)
    own_code = jnp.full((SITES_A, SITES_B, 1), 4, jnp.int32)
    return jnp.concatenate([own_code, shuffled], axis=2)


def draw_pattern(key, part):
    return draw_codes(jax.random.fold_in(key, 11))


def draw_retained(key, part):
    return draw_codes(jax.random.fold_in(key, 23))


def draw_noise(noise_key, shape):
    return jax.random.normal(noise_key, shape, jnp.float32) * 0.015


def draw_density(key, part):
    codes = draw_codes(jax.random.fold_in(key, 11))
    base_key = jax.random.fold_in(key, 37)
    self_key = jax.random.fold_in(key, 43)
    level_key = jax.random.fold_in(key, 41)
    base = draw_noise(base_key, (SITES_A, SITES_B, 4, BLOCK, BLOCK))
    raw_self = draw_noise(self_key, (SITES_A, SITES_B, BLOCK, BLOCK))
    levels = jax.random.uniform(level_key, (SITES_A, SITES_B, BLOCK), jnp.float32, 0.1, 0.9)
    identity = jnp.eye(BLOCK, dtype=jnp.float32)
    self_block = (raw_self + jnp.swapaxes(raw_self, 2, 3)) * 0.70710678 + levels[:, :, :, None] * identity[None, None, :, :]
    slots = []
    for slot_idx in range(SLOTS):
        code_here = codes[:, :, slot_idx][:, :, None, None]
        chosen = jnp.where(code_here == 4, self_block, 0.0)
        for code_low in range(4):
            chosen = jnp.where(code_here == code_low, base[:, :, code_low], chosen)
            code_high = 8 - code_low
            shift_a = code_high // 3 - 1
            shift_b = code_high % 3 - 1
            moved = jnp.roll(base[:, :, code_low], (-shift_a, -shift_b), axis=(0, 1))
            chosen = jnp.where(code_here == code_high, jnp.swapaxes(moved, 2, 3), chosen)
        slots.append(chosen)
    return jnp.stack(slots, axis=2)


def setup_inputs(seed: int = 0) -> dict:
    key_list = jax.random.split(jax.random.key(seed), 4)
    return {
        "density": draw_density(jax.random.fold_in(key_list[3], 71), 0),
        "pattern": draw_pattern(jax.random.fold_in(key_list[3], 71), 0),
        "retained": draw_retained(jax.random.fold_in(key_list[3], 71), 0),
    }


def offsets(codes):
    return codes // 3 - 1, codes % 3 - 1


def multiply(left_blocks, left_codes, right_blocks, right_codes, out_codes):
    lattice_a = left_codes.shape[0]
    lattice_b = left_codes.shape[1]
    slot_count = left_codes.shape[2]
    columns_b = jnp.arange(lattice_b, dtype=jnp.int32)
    out_a, out_b = offsets(out_codes)

    def one_row(index_a):
        row_blocks = left_blocks[index_a]
        row_codes = left_codes[index_a]
        row_out_a = out_a[index_a]
        row_out_b = out_b[index_a]
        summed = jnp.zeros(row_blocks.shape, jnp.float32)
        for slot_idx in range(slot_count):
            step_a, step_b = offsets(row_codes[:, slot_idx])
            near_a = ((index_a + step_a) % lattice_a).astype(jnp.int32)
            near_b = ((columns_b + step_b) % lattice_b).astype(jnp.int32)
            near_blocks = right_blocks[near_a, near_b]
            their_a, their_b = offsets(right_codes[near_a, near_b])
            reach_a = step_a[:, None] + their_a
            reach_b = step_b[:, None] + their_b
            matches = ((reach_a[:, :, None] == row_out_a[:, None, :]) & (reach_b[:, :, None] == row_out_b[:, None, :])).astype(jnp.float32)
            products = jnp.einsum("xij,xtjk->xtik", row_blocks[:, slot_idx], near_blocks, precision=lax.Precision.HIGHEST)
            summed = summed + jnp.einsum("xtu,xtik->xuik", matches, products, precision=lax.Precision.HIGHEST)
        return summed

    return lax.map(one_row, jnp.arange(lattice_a, dtype=jnp.int32))


def reference(density, pattern, retained):
    iterate = density
    codes = pattern
    for iteration in range(STEPS):
        square = multiply(iterate, codes, iterate, codes, retained)
        cubed = multiply(square, retained, iterate, codes, retained)
        iterate = 3.0 * square - 2.0 * cubed
        codes = retained
    return iterate
```

```python
import jax
import jax.numpy as jnp
from jax import lax
from jax.experimental import pallas as pl
from jax.experimental.pallas import tpu as pltpu
from jax.sharding import PartitionSpec as P

SLOTS = 4
SITES = 2
WIDE = SITES + 2
CHUNKS = 2
ZERO_BLOCK = 3 * WIDE * SLOTS
MESH = pl.DeviceIdType.MESH


def split(x):
    high = x.astype(jnp.bfloat16)
    low = (x - high.astype(jnp.float32)).astype(jnp.bfloat16)
    return high, low


def kernel(
    rows, cols, codes_ref, density_ref, out_ref,
    near0, near1, codes, scalars, table, right_high, right_low,
    send_sem, recv_sem, code_send, code_recv, local_sem,
):
    block = out_ref.shape[-1]
    row, col = lax.axis_index("row"), lax.axis_index("col")
    odd = lax.rem(row, 2)
    pair = row + 1 - 2 * odd
    onward = lax.rem(row + 2 - 4 * odd + rows, rows)
    backward = lax.rem(row - 2 + 4 * odd + rows, rows)
    left, right = lax.rem(col + cols - 1, cols), lax.rem(col + 1, cols)
    paired, handed = 2 - 2 * odd, 2 * odd
    own = WIDE + 1

    load = pltpu.make_async_copy(
        density_ref, near0.at[pl.ds(own * SLOTS, SITES * SLOTS)], local_sem
    )
    load.start()
    for j in range(SITES):
        codes[own + j] = codes_ref[j]
    near0[ZERO_BLOCK] = jnp.zeros((block, block), jnp.float32)
    near1[ZERO_BLOCK] = jnp.zeros((block, block), jnp.float32)

    barrier = pltpu.get_barrier_semaphore()
    others = [(pair, col), (onward, col), (backward, col), (row, left), (row, right)]
    for other in others:
        pl.semaphore_signal(barrier, inc=1, device_id=other, device_id_type=MESH)
    pl.semaphore_wait(barrier, len(others))

    def send(ref, source, target, size, sems, index, device):
        return pltpu.make_async_remote_copy(
            src_ref=ref.at[pl.ds(source, size)],
            dst_ref=ref.at[pl.ds(target, size)],
            send_sem=sems[0].at[index],
            recv_sem=sems[1].at[index],
            device_id=device,
            device_id_type=MESH,
        )

    def code_copy(index, source, target, size, device):
        return send(codes, source, target, size, (code_send, code_recv), index, device)

    part = SLOTS // CHUNKS

    def block_copy(step, kind, chunk, source, target, device):
        near = (near0, near1)[step]
        index = (step * 10 + kind) * CHUNKS + chunk
        return send(
            near, source * SLOTS + chunk * part, target * SLOTS + chunk * part, part,
            (send_sem, recv_sem), index, device,
        )

    def to_pair(step, j, chunk):
        return block_copy(step, j, chunk, own + j, handed * WIDE + 1 + j, (pair, col))

    def hand_on(step, j, chunk):
        return block_copy(
            step, 2 + j, chunk, paired * WIDE + 1 + j, handed * WIDE + 1 + j, (onward, col)
        )

    def sideways(step, place, j, chunk):
        window_row = (1, paired, handed)[place]
        device = (row, (left, right)[j])
        return block_copy(
            step, 4 + 2 * place + j, chunk,
            window_row * WIDE + 1 + j, window_row * WIDE + (WIDE - 1, 0)[j], device,
        )

    def begin(step, j):
        for chunk in range(CHUNKS):
            to_pair(step, j, chunk).start()
            sideways(step, 0, j, chunk).start()

    def relay(step):
        for j in range(SITES):
            for chunk in range(CHUNKS):
                to_pair(step, j, chunk).wait_recv()
                hand_on(step, j, chunk).start()
                sideways(step, 1, j, chunk).start()
        for j in range(SITES):
            for chunk in range(CHUNKS):
                hand_on(step, j, chunk).wait_recv()
                sideways(step, 2, j, chunk).start()

    def finish(step):
        for j in range(SITES):
            for chunk in range(CHUNKS):
                for place in range(3):
                    sideways(step, place, j, chunk).wait_recv()
        for j in range(SITES):
            for chunk in range(CHUNKS):
                to_pair(step, j, chunk).wait_send()
                hand_on(step, j, chunk).wait_send()
                for place in range(3):
                    sideways(step, place, j, chunk).wait_send()

    codes_pair = code_copy(0, own, handed * WIDE + 1, SITES, (pair, col))
    codes_on = code_copy(1, paired * WIDE + 1, handed * WIDE + 1, SITES, (onward, col))
    codes_side = [
        [
            code_copy(
                2 + 2 * place + j, window_row * WIDE + 1 + j,
                window_row * WIDE + (WIDE - 1, 0)[j], 1, (row, (left, right)[j]),
            )
            for j in range(SITES)
        ]
        for place, window_row in enumerate((1, paired, handed))
    ]
    codes_pair.start()
    for copy in codes_side[0]:
        copy.start()
    load.wait()
    for j in range(SITES):
        begin(0, j)
    codes_pair.wait_recv()
    codes_on.start()
    for copy in codes_side[1]:
        copy.start()
    codes_on.wait_recv()
    for copy in codes_side[2]:
        copy.start()
    relay(0)
    for place in range(3):
        for copy in codes_side[place]:
            copy.wait()
    codes_pair.wait_send()
    codes_on.wait_send()
    to_scalars = pltpu.make_async_copy(codes, scalars, local_sem)
    to_scalars.start()
    to_scalars.wait()

    def fill(number, left_base, right_base):
        for j in range(SITES):
            for s in range(SLOTS):
                first = scalars[own + j, 0, left_base + s]
                site = own + j + scalars[own + j, 0, 8 + left_base + s]
                second = [scalars[site, 0, right_base + t] for t in range(SLOTS)]
                for u in range(SLOTS):
                    rest = scalars[own + j, 0, 4 + u] - first
                    found = jnp.int32(ZERO_BLOCK)
                    for t in range(SLOTS):
                        found = jnp.where(second[t] == rest, site * SLOTS + t, found)
                    table[((number * SITES + j) * SLOTS + s) * SLOTS + u] = found

    fill(0, 0, 0)
    fill(1, 4, 0)
    fill(2, 4, 4)
    finish(0)

    def gather(near, number, j):
        for s in range(SLOTS):
            for u in range(SLOTS):
                found = table[((number * SITES + j) * SLOTS + s) * SLOTS + u]
                high, low = split(near[found])
                place = (pl.ds(s * block, block), pl.ds(u * block, block))
                right_high[place] = high
                right_low[place] = low

    def product(left_blocks):
        high, low = split(left_blocks)
        dot = lambda a, b: jnp.dot(a, b, preferred_element_type=jnp.float32)
        return (
            dot(high, right_low[...]) + dot(low, right_high[...]) + dot(high, right_high[...])
        )

    def purify(near, numbers, j):
        gather(near, numbers[0], j)
        mine = jnp.concatenate(
            [near[(own + j) * SLOTS + s] for s in range(SLOTS)], axis=1
        )
        square = product(mine)
        if numbers[1] != numbers[0]:
            gather(near, numbers[1], j)
        return 3.0 * square - 2.0 * product(square)

    for j in range(SITES):
        result = purify(near0, (0, 1), j)
        for u in range(SLOTS):
            near1[(own + j) * SLOTS + u] = result[:, u * block:(u + 1) * block]
        begin(1, j)
    relay(1)
    finish(1)
    for j in range(SITES):
        result = purify(near1, (2, 2), j)
        for u in range(SLOTS):
            out_ref[j * SLOTS + u] = result[:, u * block:(u + 1) * block]


def on_device(rows, cols, density, pattern, retained):
    block = density.shape[-1]
    both = jnp.concatenate([pattern, retained], axis=-1).reshape(SITES, 2 * SLOTS)
    step_a, step_b = both // 3 - 1, both % 3 - 1
    lanes = jnp.concatenate([5 * step_a + step_b, WIDE * step_a + step_b], axis=-1)
    codes = jnp.zeros((SITES, 8, 128), jnp.int32).at[:, 0, :4 * SLOTS].set(lanes)
    window = (ZERO_BLOCK + 1, block, block)
    out = pl.pallas_call(
        lambda *refs: kernel(rows, cols, *refs),
        out_shape=jax.ShapeDtypeStruct((SITES * SLOTS, block, block), jnp.float32),
        in_specs=[
            pl.BlockSpec(memory_space=pltpu.VMEM),
            pl.BlockSpec(memory_space=pl.ANY),
        ],
        out_specs=pl.BlockSpec(memory_space=pltpu.VMEM),
        scratch_shapes=[
            pltpu.VMEM(window, jnp.float32),
            pltpu.VMEM(window, jnp.float32),
            pltpu.VMEM((3 * WIDE, 8, 128), jnp.int32),
            pltpu.SMEM((3 * WIDE, 8, 128), jnp.int32),
            pltpu.SMEM((3 * SITES * SLOTS * SLOTS,), jnp.int32),
            pltpu.VMEM((SLOTS * block, SLOTS * block), jnp.bfloat16),
            pltpu.VMEM((SLOTS * block, SLOTS * block), jnp.bfloat16),
            pltpu.SemaphoreType.DMA((20 * CHUNKS,)),
            pltpu.SemaphoreType.DMA((20 * CHUNKS,)),
            pltpu.SemaphoreType.DMA((8,)),
            pltpu.SemaphoreType.DMA((8,)),
            pltpu.SemaphoreType.DMA,
        ],
        compiler_params=pltpu.CompilerParams(
            collective_id=0, has_side_effects=True, vmem_limit_bytes=32 * 1024 * 1024
        ),
    )(codes, density.reshape((SITES * SLOTS, block, block)))
    return out.reshape(density.shape)


def solution(mesh):
    rows, cols = mesh.shape["row"], mesh.shape["col"]
    return jax.shard_map(
        lambda *args: on_device(rows, cols, *args),
        mesh=mesh,
        in_specs=(P("row", "col", None, None, None), P("row", "col", None), P("row", "col", None)),
        out_specs=P("row", "col", None, None, None),
        check_vma=False,
    )
```

```python
import jax
import jax.numpy as jnp
from jax import lax
from jax.experimental import pallas as pl
from jax.experimental.pallas import tpu as pltpu
from jax.sharding import PartitionSpec as P

SLOTS = 4
SITES = 2
WIDE = SITES + 2
CHUNKS = 2
ZERO_BLOCK = 3 * WIDE * SLOTS
FLIPPED = ZERO_BLOCK + 1
MESH = pl.DeviceIdType.MESH


def split(x):
    high = x.astype(jnp.bfloat16)
    low = (x - high.astype(jnp.float32)).astype(jnp.bfloat16)
    return high, low


def kernel(
    rows, cols, pattern_ref, retained_ref, density_ref, out_ref,
    near0, near1, held, packed, codes, scalars, table, right_high, right_low,
    send_sem, recv_sem, code_send, code_recv, local_sem,
):
    block = out_ref.shape[-1]
    row, col = lax.axis_index("row"), lax.axis_index("col")
    odd, core = lax.rem(row, 2), lax.rem(col, 2)
    pair = row + 1 - 2 * odd
    onward = lax.rem(row + 2 - 4 * odd + rows, rows)
    backward = lax.rem(row - 2 + 4 * odd + rows, rows)
    beside = (lax.rem(col + cols - 1 + 2 * core, cols), lax.rem(col + cols + 1 - 2 * core, cols))
    here, there = (1 + core, 2 - core), (WIDE - 1 - 3 * core, 3 * core)
    outer_in = 3 * core
    paired, handed = 2 - 2 * odd, 2 * odd
    window_rows = (1, paired, handed)
    own = WIDE + 1

    load = pltpu.make_async_copy(
        density_ref, near0.at[pl.ds(own * SLOTS, SITES * SLOTS)], local_sem.at[0]
    )
    load.start()
    load_held = pltpu.make_async_copy(
        density_ref, held.at[pl.ds(0, SITES * SLOTS)], local_sem.at[2]
    )
    load_held.start()
    held[SITES * SLOTS] = jnp.zeros((block, block), jnp.float32)
    for j in range(SITES):
        codes[own + j] = jnp.zeros(codes.shape[1:], jnp.int32)
        for k, ref in enumerate((pattern_ref, retained_ref)):
            code = ref[j:j + 1, :]
            third = jnp.where(code >= 6, 2, jnp.where(code >= 3, 1, 0))
            codes[own + j, k:k + 1, 0:SLOTS] = code + 2 * third - 6
            codes[own + j, 2 + k:3 + k, 0:SLOTS] = code + third - 5
    own_scalars = pltpu.make_async_copy(
        codes.at[pl.ds(own, SITES)], scalars.at[pl.ds(own, SITES)], local_sem.at[1]
    )
    own_scalars.start()
    near0[ZERO_BLOCK] = jnp.zeros((block, block), jnp.float32)
    near1[ZERO_BLOCK] = jnp.zeros((block, block), jnp.float32)

    barrier = pltpu.get_barrier_semaphore()
    others = [(pair, col), (onward, col), (backward, col), (row, beside[0]), (row, beside[1])]
    for other in others:
        pl.semaphore_signal(barrier, inc=1, device_id=other, device_id_type=MESH)
    pl.semaphore_wait(barrier, len(others))

    def send(from_ref, ref, source, target, size, sems, index, device):
        return pltpu.make_async_remote_copy(
            src_ref=from_ref.at[pl.ds(source, size)],
            dst_ref=ref.at[pl.ds(target, size)],
            send_sem=sems[0].at[index],
            recv_sem=sems[1].at[index],
            device_id=device,
            device_id_type=MESH,
        )

    def code_copy(index, source, target, size, device):
        return send(codes, codes, source, target, size, (code_send, code_recv), index, device)

    def block_copy(step, kind, chunk, part, source, target, device, from_ref=None, start=None):
        near = (near0, near1)[step]
        index = (step * 11 + kind) * CHUNKS + chunk
        first = source * SLOTS + chunk * part if start is None else start
        return send(
            near if from_ref is None else from_ref, near, first, target * SLOTS + chunk * part,
            part, (send_sem, recv_sem), index, device,
        )

    parts = (2 // CHUNKS, SLOTS // CHUNKS)

    def to_pair(step, role, chunk):
        column, part = here[role], parts[step]
        target = handed * WIDE + column
        if step == 0:
            start = (column - 1) * 2 + chunk * part
            return block_copy(0, role, chunk, part, 0, target, (pair, col), packed, start)
        return block_copy(1, role, chunk, part, WIDE + column, target, (pair, col))

    def hand_on(step, role, chunk):
        column = (here + (outer_in,))[role]
        return block_copy(
            step, 2 + role, chunk, parts[step],
            paired * WIDE + column, handed * WIDE + column, (onward, col),
        )

    def sideways(step, place, role, chunk):
        part = SLOTS // CHUNKS if place == 0 else parts[step]
        base = window_rows[place] * WIDE
        return block_copy(
            step, 5 + 2 * place + role, chunk, part,
            base + here[role], base + there[role], (row, beside[role]),
        )

    def begin(step, role):
        for chunk in range(CHUNKS):
            to_pair(step, role, chunk).start()
        for chunk in range(CHUNKS):
            sideways(step, 0, role, chunk).start()

    def relay(step):
        for role in range(2):
            for chunk in range(CHUNKS):
                to_pair(step, role, chunk).wait_recv()
                hand_on(step, role, chunk).start()
                sideways(step, 1, role, chunk).start()
        hand_on(step, 0, 0).wait_recv()
        sideways(step, 2, 0, 0).start()
        sideways(step, 1, 0, 1).wait_recv()
        hand_on(step, 2, 1).start()
        hand_on(step, 0, 1).wait_recv()
        for chunk in range(CHUNKS):
            hand_on(step, 1, chunk).wait_recv()
            sideways(step, 2, 1, chunk).start()

    def finish(step):
        for chunk in range(CHUNKS):
            for role in range(2):
                sideways(step, 0, role, chunk).wait_recv()
        sideways(step, 1, 0, 0).wait_recv()
        sideways(step, 2, 0, 0).wait_recv()
        hand_on(step, 2, 1).wait_recv()
        for chunk in range(CHUNKS):
            for place in (1, 2):
                sideways(step, place, 1, chunk).wait_recv()
        for chunk in range(CHUNKS):
            for role in range(2):
                to_pair(step, role, chunk).wait_send()
                hand_on(step, role, chunk).wait_send()
                for place in range(3):
                    if (place, role, chunk) != (2, 0, 1):
                        sideways(step, place, role, chunk).wait_send()
        hand_on(step, 2, 1).wait_send()

    def flip(source, target):
        near0[target] = near0[source].T

    codes_pair = code_copy(0, own, handed * WIDE + 1, SITES, (pair, col))
    codes_on = code_copy(1, paired * WIDE + 1, handed * WIDE + 1, SITES, (onward, col))
    codes_side = [
        [
            code_copy(
                2 + 2 * place + role, window_row * WIDE + here[role],
                window_row * WIDE + there[role], 1, (row, beside[role]),
            )
            for role in range(2)
        ]
        for place, window_row in enumerate(window_rows)
    ]
    codes_pair.start()
    for copy in codes_side[0]:
        copy.start()
    own_scalars.wait()
    load_held.wait()
    for j in range(SITES):
        packed[2 * j] = held[j * SLOTS]
        found = jnp.int32(SITES * SLOTS)
        for t in range(1, SLOTS):
            found = jnp.where(scalars[own + j, 0, t] == 1, j * SLOTS + t, found)
        packed[2 * j + 1] = held[found]
    load.wait()
    for role in range(2):
        begin(0, role)
    for j in range(SITES):
        for t in range(1, SLOTS):
            flip((own + j) * SLOTS + t, FLIPPED + (1 + j) * SLOTS + t)
    codes_pair.wait_recv()
    codes_on.start()
    for copy in codes_side[1]:
        copy.start()
    codes_on.wait_recv()
    for copy in codes_side[2]:
        copy.start()
    relay(0)
    for place in range(3):
        for copy in codes_side[place]:
            copy.wait()
    codes_pair.wait_send()
    codes_on.wait_send()
    to_scalars = pltpu.make_async_copy(codes, scalars, local_sem.at[1])
    to_scalars.start()
    to_scalars.wait()

    def fill(number, left_row, right_row, symmetric):
        def one(j, s):
            first = scalars[own + j, left_row, s]
            site = own + j + scalars[own + j, 2 + left_row, s]
            second = [scalars[site, right_row, t] for t in range(SLOTS)]
            in_row = (site >= WIDE) & (site < 2 * WIDE)
            for u in range(SLOTS):
                rest = scalars[own + j, 1, u] - first
                found = jnp.int32(ZERO_BLOCK)
                for t in range(SLOTS):
                    found = jnp.where(second[t] == rest, site * SLOTS + t, found)
                if symmetric:
                    last = own + j + scalars[own + j, 3, u]
                    reverse = jnp.int32(ZERO_BLOCK)
                    for t in range(SLOTS):
                        reverse = jnp.where(
                            scalars[last, right_row, t] == -rest,
                            FLIPPED + (last - WIDE) * SLOTS + t, reverse,
                        )
                    last_in_row = (last >= WIDE) & (last < 2 * WIDE)
                    edge = FLIPPED + WIDE * SLOTS + jnp.where(last < WIDE, last, last - WIDE)
                    sent = jnp.where(
                        rest == 0, site * SLOTS,
                        jnp.where(rest == 1, site * SLOTS + 1, jnp.where(rest == -1, edge, reverse)),
                    )
                    usable = (found != ZERO_BLOCK) & (
                        last_in_row | (rest == 0) | (rest == 1) | (rest == -1)
                    )
                    sent = jnp.where(usable, sent, ZERO_BLOCK)
                    found = jnp.where(in_row, found, sent)
                table[((number * SITES + j) * SLOTS + s) * SLOTS + u] = found

        for j in range(SITES):
            for s in range(SLOTS):
                one(j, s)

    fill(0, 0, 0, True)
    fill(1, 1, 0, True)
    fill(2, 1, 1, False)
    finish(0)
    for column in (0, WIDE - 1):
        for t in range(1, SLOTS):
            flip((WIDE + column) * SLOTS + t, FLIPPED + column * SLOTS + t)
    for k in range(2):
        for column in range(WIDE - 1):
            flip((2 * k * WIDE + column) * SLOTS + 1, FLIPPED + (SLOTS + k) * WIDE + column)

    def gather(near, number, j):
        for s in range(SLOTS):
            for u in range(SLOTS):
                found = table[((number * SITES + j) * SLOTS + s) * SLOTS + u]
                high, low = split(near[found])
                place = (pl.ds(s * block, block), pl.ds(u * block, block))
                right_high[place] = high
                right_low[place] = low

    def product(left_blocks):
        high, low = split(left_blocks)
        dot = lambda a, b: jnp.dot(a, b, preferred_element_type=jnp.float32)
        return (
            dot(high, right_low[...]) + dot(low, right_high[...]) + dot(high, right_high[...])
        )

    def purify(near, numbers, j):
        gather(near, numbers[0], j)
        mine = jnp.concatenate(
            [near[(own + j) * SLOTS + s] for s in range(SLOTS)], axis=1
        )
        square = product(mine)
        if numbers[1] != numbers[0]:
            gather(near, numbers[1], j)
        return 3.0 * square - 2.0 * product(square)

    for role in range(2):
        j = here[role] - 1
        result = purify(near0, (0, 1), j)
        for u in range(SLOTS):
            near1[(own + j) * SLOTS + u] = result[:, u * block:(u + 1) * block]
        begin(1, role)
    relay(1)
    finish(1)
    for j in range(SITES):
        result = purify(near1, (2, 2), j)
        for u in range(SLOTS):
            out_ref[j * SLOTS + u] = result[:, u * block:(u + 1) * block]


def on_device(rows, cols, density, pattern, retained):
    block = density.shape[-1]
    vmem = pl.BlockSpec(memory_space=pltpu.VMEM)
    out = pl.pallas_call(
        lambda *refs: kernel(rows, cols, *refs),
        out_shape=jax.ShapeDtypeStruct((SITES * SLOTS, block, block), jnp.float32),
        in_specs=[vmem, vmem, pl.BlockSpec(memory_space=pl.ANY)],
        out_specs=vmem,
        scratch_shapes=[
            pltpu.VMEM((FLIPPED + WIDE * SLOTS + 2 * WIDE, block, block), jnp.float32),
            pltpu.VMEM((ZERO_BLOCK + 1, block, block), jnp.float32),
            pltpu.VMEM((SITES * SLOTS + 1, block, block), jnp.float32),
            pltpu.VMEM((2 * SITES, block, block), jnp.float32),
            pltpu.VMEM((3 * WIDE, 8, 128), jnp.int32),
            pltpu.SMEM((3 * WIDE, 8, 128), jnp.int32),
            pltpu.SMEM((3 * SITES * SLOTS * SLOTS,), jnp.int32),
            pltpu.VMEM((SLOTS * block, SLOTS * block), jnp.bfloat16),
            pltpu.VMEM((SLOTS * block, SLOTS * block), jnp.bfloat16),
            pltpu.SemaphoreType.DMA((22 * CHUNKS,)),
            pltpu.SemaphoreType.DMA((22 * CHUNKS,)),
            pltpu.SemaphoreType.DMA((8,)),
            pltpu.SemaphoreType.DMA((8,)),
            pltpu.SemaphoreType.DMA((3,)),
        ],
        compiler_params=pltpu.CompilerParams(
            collective_id=0, has_side_effects=True, vmem_limit_bytes=32 * 1024 * 1024
        ),
    )(
        pattern.reshape((SITES, SLOTS)),
        retained.reshape((SITES, SLOTS)),
        density.reshape((SITES * SLOTS, block, block)),
    )
    return out.reshape(density.shape)


def solution(mesh):
    rows, cols = mesh.shape["row"], mesh.shape["col"]
    return jax.shard_map(
        lambda *args: on_device(rows, cols, *args),
        mesh=mesh,
        in_specs=(P("row", "col", None, None, None), P("row", "col", None), P("row", "col", None)),
        out_specs=P("row", "col", None, None, None),
        check_vma=False,
    )
```

```python
import jax
import jax.numpy as jnp
from jax import lax
from jax.experimental import pallas as pl
from jax.experimental.pallas import tpu as pltpu
from jax.sharding import PartitionSpec as P

SLOTS = 4
SITES = 2
WIDE = SITES + 2
CHUNKS = 2
ZERO_BLOCK = 3 * WIDE * SLOTS
FLIPPED = ZERO_BLOCK + 1
MESH = pl.DeviceIdType.MESH


def split(x):
    high = x.astype(jnp.bfloat16)
    low = (x - high.astype(jnp.float32)).astype(jnp.bfloat16)
    return high, low


def kernel(
    rows, cols, pattern_ref, retained_ref, density_ref, out_ref,
    near0, near1, far0, far1, own_codes, held, packed, codes, scalars, table, right_high, right_low,
    send_sem, recv_sem, code_send, code_recv, local_sem,
):
    block = out_ref.shape[-1]
    row, col = lax.axis_index("row"), lax.axis_index("col")
    odd, core = lax.rem(row, 2), lax.rem(col, 2)
    pair = row + 1 - 2 * odd
    onward = lax.rem(row + 2 - 4 * odd + rows, rows)
    backward = lax.rem(row - 2 + 4 * odd + rows, rows)
    beside = (lax.rem(col + cols - 1 + 2 * core, cols), lax.rem(col + cols + 1 - 2 * core, cols))
    here, there = (1 + core, 2 - core), (WIDE - 1 - 3 * core, 3 * core)
    outer_in = 3 * core
    paired, handed = 2 - 2 * odd, 2 * odd
    window_rows = (1, paired, handed)
    own = WIDE + 1

    load = pltpu.make_async_copy(
        density_ref, near0.at[pl.ds(own * SLOTS, SITES * SLOTS)], local_sem.at[0]
    )
    load.start()
    load_held = pltpu.make_async_copy(
        density_ref, held.at[pl.ds(0, SITES * SLOTS)], local_sem.at[2]
    )
    load_held.start()
    held[SITES * SLOTS] = jnp.zeros((block, block), jnp.float32)
    load_codes = [
        pltpu.make_async_copy(ref, own_codes.at[k], local_sem.at[3 + k])
        for k, ref in enumerate((pattern_ref, retained_ref))
    ]
    for copy in load_codes:
        copy.start()
    for j in range(SITES):
        codes[own + j] = jnp.zeros(codes.shape[1:], jnp.int32)
    for copy in load_codes:
        copy.wait()
    for j in range(SITES):
        for k in range(2):
            code = own_codes[k, j:j + 1, :]
            third = jnp.where(code >= 6, 2, jnp.where(code >= 3, 1, 0))
            codes[own + j, k:k + 1, 0:SLOTS] = code + 2 * third - 6
            codes[own + j, 2 + k:3 + k, 0:SLOTS] = code + third - 5
    own_scalars = pltpu.make_async_copy(
        codes.at[pl.ds(own, SITES)], scalars.at[pl.ds(own, SITES)], local_sem.at[1]
    )
    own_scalars.start()
    near0[ZERO_BLOCK] = jnp.zeros((block, block), jnp.float32)
    near1[ZERO_BLOCK] = jnp.zeros((block, block), jnp.float32)

    barrier = pltpu.get_barrier_semaphore()
    others = [(pair, col), (onward, col), (backward, col), (row, beside[0]), (row, beside[1])]
    for other in others:
        pl.semaphore_signal(barrier, inc=1, device_id=other, device_id_type=MESH)
    pl.semaphore_wait(barrier, len(others))

    def send(from_ref, ref, source, target, size, sems, index, device):
        return pltpu.make_async_remote_copy(
            src_ref=from_ref.at[pl.ds(source, size)],
            dst_ref=ref.at[pl.ds(target, size)],
            send_sem=sems[0].at[index],
            recv_sem=sems[1].at[index],
            device_id=device,
            device_id_type=MESH,
        )

    def code_copy(index, source, target, size, device):
        return send(codes, codes, source, target, size, (code_send, code_recv), index, device)

    def block_copy(step, kind, chunk, part, source, target, device, from_ref, to_ref, start=None):
        index = (step * 11 + kind) * CHUNKS + chunk
        first = source * SLOTS + chunk * part if start is None else start
        return send(
            from_ref, to_ref, first, target * SLOTS + chunk * part,
            part, (send_sem, recv_sem), index, device,
        )

    parts = (2 // CHUNKS, SLOTS // CHUNKS)
    nears, fars = (near0, near1), (far0, far1)

    def to_pair(step, role, chunk):
        column, part = here[role], parts[step]
        target = handed * WIDE + column
        if step == 0:
            start = (column - 1) * 2 + chunk * part
            return block_copy(0, role, chunk, part, 0, target, (pair, col), packed, near0, start)
        return block_copy(
            1, role, chunk, part, WIDE + column, target, (pair, col), near1, near1
        )

    def hand_on(step, role, chunk):
        near, far = nears[step], fars[step]
        if role == 2:
            return block_copy(
                step, 4, chunk, parts[step], paired, handed, (onward, col), far, far
            )
        column = here[role]
        return block_copy(
            step, 2 + role, chunk, parts[step],
            paired * WIDE + column, handed * WIDE + column, (onward, col), near, near,
        )

    def sideways(step, place, role, chunk):
        part = SLOTS // CHUNKS if place == 0 else parts[step]
        near, far = nears[step], fars[step]
        base = window_rows[place] * WIDE
        target = base + there[1] if role else window_rows[place]
        return block_copy(
            step, 5 + 2 * place + role, chunk, part,
            base + here[role], target, (row, beside[role]), near, near if role else far,
        )

    def begin(step, role):
        for chunk in range(CHUNKS):
            to_pair(step, role, chunk).start()
        for chunk in range(CHUNKS):
            sideways(step, 0, role, chunk).start()

    def relay(step):
        for role in ((0, 1), (1, 0))[step]:
            for chunk in range(CHUNKS):
                to_pair(step, role, chunk).wait_recv()
                hand_on(step, role, chunk).start()
                sideways(step, 1, role, chunk).start()

        def inner():
            for chunk in range(CHUNKS):
                hand_on(step, 1, chunk).wait_recv()
                sideways(step, 2, 1, chunk).start()

        if step == 1:
            inner()
        hand_on(step, 0, 0).wait_recv()
        sideways(step, 2, 0, 0).start()
        sideways(step, 1, 0, 1).wait_recv()
        hand_on(step, 2, 1).start()
        hand_on(step, 0, 1).wait_recv()
        if step == 0:
            inner()

    def inner_arrives(step):
        for chunk in range(CHUNKS):
            for place in range(3):
                sideways(step, place, 1, chunk).wait_recv()

    def outer_arrives(step):
        for chunk in range(CHUNKS):
            sideways(step, 0, 0, chunk).wait_recv()
        sideways(step, 1, 0, 0).wait_recv()
        sideways(step, 2, 0, 0).wait_recv()
        hand_on(step, 2, 1).wait_recv()
        near, far = nears[step], fars[step]
        for window_row in range(3):
            count = SLOTS if step == 1 or window_row == 1 else 2
            for t in range(count):
                near[(window_row * WIDE + outer_in) * SLOTS + t] = far[window_row * SLOTS + t]

    def all_sent(step):
        for chunk in range(CHUNKS):
            for role in range(2):
                to_pair(step, role, chunk).wait_send()
                hand_on(step, role, chunk).wait_send()
                for place in range(3):
                    if (place, role, chunk) != (2, 0, 1):
                        sideways(step, place, role, chunk).wait_send()
        hand_on(step, 2, 1).wait_send()

    def flip(source, target):
        near0[target] = near0[source].T

    codes_pair = code_copy(0, own, handed * WIDE + 1, SITES, (pair, col))
    codes_on = code_copy(1, paired * WIDE + 1, handed * WIDE + 1, SITES, (onward, col))
    codes_side = [
        [
            code_copy(
                2 + 2 * place + role, window_row * WIDE + here[role],
                window_row * WIDE + there[role], 1, (row, beside[role]),
            )
            for role in range(2)
        ]
        for place, window_row in enumerate(window_rows)
    ]
    codes_pair.start()
    for copy in codes_side[0]:
        copy.start()
    own_scalars.wait()
    load_held.wait()
    for j in range(SITES):
        packed[2 * j] = held[j * SLOTS]
        found = jnp.int32(SITES * SLOTS)
        for t in range(1, SLOTS):
            found = jnp.where(scalars[own + j, 0, t] == 1, j * SLOTS + t, found)
        packed[2 * j + 1] = held[found]
    load.wait()
    for role in range(2):
        begin(0, role)
    for j in range(SITES):
        for t in range(1, SLOTS):
            flip((own + j) * SLOTS + t, FLIPPED + (1 + j) * SLOTS + t)
    codes_pair.wait_recv()
    codes_on.start()
    for copy in codes_side[1]:
        copy.start()
    codes_on.wait_recv()
    for copy in codes_side[2]:
        copy.start()
    relay(0)
    for place in range(3):
        for copy in codes_side[place]:
            copy.wait()
    codes_pair.wait_send()
    codes_on.wait_send()
    to_scalars = pltpu.make_async_copy(codes, scalars, local_sem.at[1])
    to_scalars.start()
    to_scalars.wait()

    def fill(number, left_row, right_row, symmetric):
        def one(j, s):
            first = scalars[own + j, left_row, s]
            site = own + j + scalars[own + j, 2 + left_row, s]
            second = [scalars[site, right_row, t] for t in range(SLOTS)]
            in_row = (site >= WIDE) & (site < 2 * WIDE)
            for u in range(SLOTS):
                rest = scalars[own + j, 1, u] - first
                found = jnp.int32(ZERO_BLOCK)
                for t in range(SLOTS):
                    found = jnp.where(second[t] == rest, site * SLOTS + t, found)
                if symmetric:
                    last = own + j + scalars[own + j, 3, u]
                    reverse = jnp.int32(ZERO_BLOCK)
                    for t in range(SLOTS):
                        reverse = jnp.where(
                            scalars[last, right_row, t] == -rest,
                            FLIPPED + (last - WIDE) * SLOTS + t, reverse,
                        )
                    last_in_row = (last >= WIDE) & (last < 2 * WIDE)
                    edge = FLIPPED + WIDE * SLOTS + jnp.where(last < WIDE, last, last - WIDE)
                    sent = jnp.where(
                        rest == 0, site * SLOTS,
                        jnp.where(rest == 1, site * SLOTS + 1, jnp.where(rest == -1, edge, reverse)),
                    )
                    usable = (found != ZERO_BLOCK) & (
                        last_in_row | (rest == 0) | (rest == 1) | (rest == -1)
                    )
                    sent = jnp.where(usable, sent, ZERO_BLOCK)
                    found = jnp.where(in_row, found, sent)
                table[((number * SITES + j) * SLOTS + s) * SLOTS + u] = found

        for j in range(SITES):
            for s in range(SLOTS):
                one(j, s)

    fill(0, 0, 0, True)
    fill(1, 1, 0, True)

    def flip_side(column):
        for t in range(1, SLOTS):
            flip((WIDE + column) * SLOTS + t, FLIPPED + column * SLOTS + t)

    def flip_edge(column):
        for k in range(2):
            flip((2 * k * WIDE + column) * SLOTS + 1, FLIPPED + (SLOTS + k) * WIDE + column)

    def gather(near, number, j):
        for s in range(SLOTS):
            for u in range(SLOTS):
                found = table[((number * SITES + j) * SLOTS + s) * SLOTS + u]
                high, low = split(near[found])
                place = (pl.ds(s * block, block), pl.ds(u * block, block))
                right_high[place] = high
                right_low[place] = low

    def product(left_blocks):
        high, low = split(left_blocks)
        dot = lambda a, b: jnp.dot(a, b, preferred_element_type=jnp.float32)
        return (
            dot(high, right_low[...]) + dot(low, right_high[...]) + dot(high, right_high[...])
        )

    def purify(near, numbers, j):
        gather(near, numbers[0], j)
        mine = jnp.concatenate(
            [near[(own + j) * SLOTS + s] for s in range(SLOTS)], axis=1
        )
        square = product(mine)
        if numbers[1] != numbers[0]:
            gather(near, numbers[1], j)
        return 3.0 * square - 2.0 * product(square)

    def first_step(role):
        j = here[role] - 1
        result = purify(near0, (0, 1), j)
        for u in range(SLOTS):
            near1[(own + j) * SLOTS + u] = result[:, u * block:(u + 1) * block]
        begin(1, role)

    def second_step(role):
        j = here[role] - 1
        result = purify(near1, (2, 2), j)
        for u in range(SLOTS):
            out_ref[j * SLOTS + u] = result[:, u * block:(u + 1) * block]

    inner_arrives(0)
    flip_side(WIDE - 1 - outer_in)
    flip_edge(1)
    flip_edge(2 - 2 * core)
    first_step(1)
    outer_arrives(0)
    flip_side(outer_in)
    flip_edge(2 * core)
    first_step(0)
    relay(1)
    fill(2, 1, 1, False)
    inner_arrives(1)
    second_step(1)
    outer_arrives(1)
    second_step(0)
    all_sent(0)
    all_sent(1)


def on_device(rows, cols, density, pattern, retained):
    block = density.shape[-1]
    vmem = pl.BlockSpec(memory_space=pltpu.VMEM)
    out = pl.pallas_call(
        lambda *refs: kernel(rows, cols, *refs),
        out_shape=jax.ShapeDtypeStruct((SITES * SLOTS, block, block), jnp.float32),
        in_specs=[pl.BlockSpec(memory_space=pltpu.HBM)] * 3,
        out_specs=vmem,
        scratch_shapes=[
            pltpu.VMEM((FLIPPED + WIDE * SLOTS + 2 * WIDE, block, block), jnp.float32),
            pltpu.VMEM((ZERO_BLOCK + 1, block, block), jnp.float32),
            pltpu.VMEM((3 * SLOTS, block, block), jnp.float32),
            pltpu.VMEM((3 * SLOTS, block, block), jnp.float32),
            pltpu.VMEM((2, SITES, SLOTS), jnp.int32),
            pltpu.VMEM((SITES * SLOTS + 1, block, block), jnp.float32),
            pltpu.VMEM((2 * SITES, block, block), jnp.float32),
            pltpu.VMEM((3 * WIDE, 8, 128), jnp.int32),
            pltpu.SMEM((3 * WIDE, 8, 128), jnp.int32),
            pltpu.SMEM((3 * SITES * SLOTS * SLOTS,), jnp.int32),
            pltpu.VMEM((SLOTS * block, SLOTS * block), jnp.bfloat16),
            pltpu.VMEM((SLOTS * block, SLOTS * block), jnp.bfloat16),
            pltpu.SemaphoreType.DMA((22 * CHUNKS,)),
            pltpu.SemaphoreType.DMA((22 * CHUNKS,)),
            pltpu.SemaphoreType.DMA((8,)),
            pltpu.SemaphoreType.DMA((8,)),
            pltpu.SemaphoreType.DMA((5,)),
        ],
        compiler_params=pltpu.CompilerParams(
            collective_id=0, has_side_effects=True, vmem_limit_bytes=32 * 1024 * 1024
        ),
    )(
        pattern.reshape((SITES, SLOTS)),
        retained.reshape((SITES, SLOTS)),
        density.reshape((SITES * SLOTS, block, block)),
    )
    return out.reshape(density.shape)


def solution(mesh):
    rows, cols = mesh.shape["row"], mesh.shape["col"]
    return jax.shard_map(
        lambda *args: on_device(rows, cols, *args),
        mesh=mesh,
        in_specs=(P("row", "col", None, None, None), P("row", "col", None), P("row", "col", None)),
        out_specs=P("row", "col", None, None, None),
        check_vma=False,
    )
```

```python
import jax
import jax.numpy as jnp
from jax import lax
from jax.experimental import pallas as pl
from jax.experimental.pallas import tpu as pltpu
from jax.sharding import PartitionSpec as P

SLOTS = 4
SITES = 2
WIDE = SITES + 2
CHUNKS = 2
ZERO_BLOCK = 3 * WIDE * SLOTS
FLIPPED = ZERO_BLOCK + 1
MESH = pl.DeviceIdType.MESH


def split(x):
    high = x.astype(jnp.bfloat16)
    low = (x - high.astype(jnp.float32)).astype(jnp.bfloat16)
    return high, low


def kernel(
    rows, cols, pattern_ref, retained_ref, density_ref, out_ref,
    near0, near1, far0, far1, own_codes, held, packed, codes, scalars, table, right_high, right_low,
    send_sem, recv_sem, code_send, code_recv, local_sem,
):
    block = out_ref.shape[-1]
    row, col = lax.axis_index("row"), lax.axis_index("col")
    odd, core = lax.rem(row, 2), lax.rem(col, 2)
    pair = row + 1 - 2 * odd
    onward = lax.rem(row + 2 - 4 * odd + rows, rows)
    backward = lax.rem(row - 2 + 4 * odd + rows, rows)
    beside = (lax.rem(col + cols - 1 + 2 * core, cols), lax.rem(col + cols + 1 - 2 * core, cols))
    here, there = (1 + core, 2 - core), (WIDE - 1 - 3 * core, 3 * core)
    outer_in = 3 * core
    paired, handed = 2 - 2 * odd, 2 * odd
    window_rows = (1, paired, handed)
    own = WIDE + 1

    load = pltpu.make_async_copy(
        density_ref, near0.at[pl.ds(own * SLOTS, SITES * SLOTS)], local_sem.at[0]
    )
    load.start()
    load_held = pltpu.make_async_copy(
        density_ref, held.at[pl.ds(0, SITES * SLOTS)], local_sem.at[2]
    )
    load_held.start()
    held[SITES * SLOTS] = jnp.zeros((block, block), jnp.float32)
    load_codes = [
        pltpu.make_async_copy(ref, own_codes.at[k], local_sem.at[3 + k])
        for k, ref in enumerate((pattern_ref, retained_ref))
    ]
    for copy in load_codes:
        copy.start()
    for j in range(SITES):
        codes[own + j] = jnp.zeros(codes.shape[1:], jnp.int32)
    for copy in load_codes:
        copy.wait()
    for j in range(SITES):
        for k in range(2):
            code = own_codes[k, j:j + 1, :]
            third = jnp.where(code >= 6, 2, jnp.where(code >= 3, 1, 0))
            codes[own + j, k:k + 1, 0:SLOTS] = code + 2 * third - 6
            codes[own + j, 2 + k:3 + k, 0:SLOTS] = code + third - 5
    own_scalars = pltpu.make_async_copy(
        codes.at[pl.ds(own, SITES)], scalars.at[pl.ds(own, SITES)], local_sem.at[1]
    )
    own_scalars.start()
    near0[ZERO_BLOCK] = jnp.zeros((block, block), jnp.float32)
    near1[ZERO_BLOCK] = jnp.zeros((block, block), jnp.float32)

    barrier = pltpu.get_barrier_semaphore()
    others = [(pair, col), (onward, col), (backward, col), (row, beside[0]), (row, beside[1])]
    for other in others:
        pl.semaphore_signal(barrier, inc=1, device_id=other, device_id_type=MESH)
    pl.semaphore_wait(barrier, len(others))

    def send(from_ref, ref, source, target, size, sems, index, device):
        return pltpu.make_async_remote_copy(
            src_ref=from_ref.at[pl.ds(source, size)],
            dst_ref=ref.at[pl.ds(target, size)],
            send_sem=sems[0].at[index],
            recv_sem=sems[1].at[index],
            device_id=device,
            device_id_type=MESH,
        )

    def code_copy(index, source, target, size, device):
        return send(codes, codes, source, target, size, (code_send, code_recv), index, device)

    def block_copy(step, kind, chunk, part, source, target, device, from_ref, to_ref, start=None):
        index = (step * 11 + kind) * CHUNKS + chunk
        first = source * SLOTS + chunk * part if start is None else start
        return send(
            from_ref, to_ref, first, target * SLOTS + chunk * part,
            part, (send_sem, recv_sem), index, device,
        )

    parts = (2 // CHUNKS, SLOTS // CHUNKS)
    nears, fars = (near0, near1), (far0, far1)

    def to_pair(step, role, chunk):
        column, part = here[role], parts[step]
        target = handed * WIDE + column
        if step == 0:
            start = (column - 1) * 2 + chunk * part
            return block_copy(0, role, chunk, part, 0, target, (pair, col), packed, near0, start)
        return block_copy(
            1, role, chunk, part, WIDE + column, target, (pair, col), near1, near1
        )

    def hand_on(step, role, chunk):
        near, far = nears[step], fars[step]
        if role == 2:
            return block_copy(
                step, 4, chunk, parts[step], paired, handed, (onward, col), far, far
            )
        column = here[role]
        return block_copy(
            step, 2 + role, chunk, parts[step],
            paired * WIDE + column, handed * WIDE + column, (onward, col), near, near,
        )

    def sideways(step, place, role, chunk):
        part = SLOTS // CHUNKS if place == 0 else parts[step]
        near, far = nears[step], fars[step]
        base = window_rows[place] * WIDE
        target = base + there[1] if role else window_rows[place]
        return block_copy(
            step, 5 + 2 * place + role, chunk, part,
            base + here[role], target, (row, beside[role]), near, near if role else far,
        )

    def begin(step, role):
        for chunk in range(CHUNKS):
            to_pair(step, role, chunk).start()
        for chunk in range(CHUNKS):
            sideways(step, 0, role, chunk).start()

    def relay(step):
        for role in ((0, 1), (1, 0))[step]:
            for chunk in range(CHUNKS):
                to_pair(step, role, chunk).wait_recv()
                hand_on(step, role, chunk).start()
                sideways(step, 1, role, chunk).start()

        def inner():
            for chunk in range(CHUNKS):
                hand_on(step, 1, chunk).wait_recv()
                sideways(step, 2, 1, chunk).start()

        if step == 1:
            inner()
        hand_on(step, 0, 0).wait_recv()
        sideways(step, 2, 0, 0).start()
        sideways(step, 1, 0, 1).wait_recv()
        hand_on(step, 2, 1).start()
        hand_on(step, 0, 1).wait_recv()
        if step == 0:
            inner()

    def inner_arrives(step):
        for chunk in range(CHUNKS):
            for place in range(3):
                sideways(step, place, 1, chunk).wait_recv()

    def outer_arrives(step):
        for chunk in range(CHUNKS):
            sideways(step, 0, 0, chunk).wait_recv()
        sideways(step, 1, 0, 0).wait_recv()
        sideways(step, 2, 0, 0).wait_recv()
        hand_on(step, 2, 1).wait_recv()
        near, far = nears[step], fars[step]
        for window_row in range(3):
            count = SLOTS if step == 1 or window_row == 1 else 2
            for t in range(count):
                near[(window_row * WIDE + outer_in) * SLOTS + t] = far[window_row * SLOTS + t]

    def all_sent(step):
        for chunk in range(CHUNKS):
            for role in range(2):
                to_pair(step, role, chunk).wait_send()
                hand_on(step, role, chunk).wait_send()
                for place in range(3):
                    if (place, role, chunk) != (2, 0, 1):
                        sideways(step, place, role, chunk).wait_send()
        hand_on(step, 2, 1).wait_send()

    def flip(source, target):
        near0[target] = near0[source].T

    codes_pair = code_copy(0, own, handed * WIDE + 1, SITES, (pair, col))
    codes_on = code_copy(1, paired * WIDE + 1, handed * WIDE + 1, SITES, (onward, col))
    codes_side = [
        [
            code_copy(
                2 + 2 * place + role, window_row * WIDE + here[role],
                window_row * WIDE + there[role], 1, (row, beside[role]),
            )
            for role in range(2)
        ]
        for place, window_row in enumerate(window_rows)
    ]
    codes_pair.start()
    for copy in codes_side[0]:
        copy.start()
    own_scalars.wait()
    load_held.wait()
    for j in range(SITES):
        packed[2 * j] = held[j * SLOTS]
        found = jnp.int32(SITES * SLOTS)
        for t in range(1, SLOTS):
            found = jnp.where(scalars[own + j, 0, t] == 1, j * SLOTS + t, found)
        packed[2 * j + 1] = held[found]
    load.wait()
    for role in range(2):
        begin(0, role)
    for j in range(SITES):
        for t in range(1, SLOTS):
            flip((own + j) * SLOTS + t, FLIPPED + (1 + j) * SLOTS + t)
    codes_pair.wait_recv()
    codes_on.start()
    for copy in codes_side[1]:
        copy.start()
    codes_on.wait_recv()
    for copy in codes_side[2]:
        copy.start()
    relay(0)
    for place in range(3):
        for copy in codes_side[place]:
            copy.wait()
    codes_pair.wait_send()
    codes_on.wait_send()
    to_scalars = pltpu.make_async_copy(codes, scalars, local_sem.at[1])
    to_scalars.start()
    to_scalars.wait()

    def fill(number, left_row, right_row, symmetric):
        def one(j, s):
            first = scalars[own + j, left_row, s]
            site = own + j + scalars[own + j, 2 + left_row, s]
            second = [scalars[site, right_row, t] for t in range(SLOTS)]
            in_row = (site >= WIDE) & (site < 2 * WIDE)
            for u in range(SLOTS):
                rest = scalars[own + j, 1, u] - first
                found = jnp.int32(ZERO_BLOCK)
                for t in range(SLOTS):
                    found = jnp.where(second[t] == rest, site * SLOTS + t, found)
                if symmetric:
                    last = own + j + scalars[own + j, 3, u]
                    reverse = jnp.int32(ZERO_BLOCK)
                    for t in range(SLOTS):
                        reverse = jnp.where(
                            scalars[last, right_row, t] == -rest,
                            FLIPPED + (last - WIDE) * SLOTS + t, reverse,
                        )
                    last_in_row = (last >= WIDE) & (last < 2 * WIDE)
                    edge = FLIPPED + WIDE * SLOTS + jnp.where(last < WIDE, last, last - WIDE)
                    sent = jnp.where(
                        rest == 0, site * SLOTS,
                        jnp.where(rest == 1, site * SLOTS + 1, jnp.where(rest == -1, edge, reverse)),
                    )
                    usable = (found != ZERO_BLOCK) & (
                        last_in_row | (rest == 0) | (rest == 1) | (rest == -1)
                    )
                    sent = jnp.where(usable, sent, ZERO_BLOCK)
                    found = jnp.where(in_row, found, sent)
                table[((number * SITES + j) * SLOTS + s) * SLOTS + u] = found

        for j in range(SITES):
            for s in range(SLOTS):
                one(j, s)

    fill(0, 0, 0, True)
    fill(1, 1, 0, True)

    def flip_side(column):
        for t in range(1, SLOTS):
            flip((WIDE + column) * SLOTS + t, FLIPPED + column * SLOTS + t)

    def flip_edge(column):
        for k in range(2):
            flip((2 * k * WIDE + column) * SLOTS + 1, FLIPPED + (SLOTS + k) * WIDE + column)

    def gather(near, number, j):
        for s in range(SLOTS):
            for u in range(SLOTS):
                found = table[((number * SITES + j) * SLOTS + s) * SLOTS + u]
                high, low = split(near[found])
                place = (pl.ds(s * block, block), pl.ds(u * block, block))
                right_high[place] = high
                right_low[place] = low

    def product(left_blocks):
        high, low = split(left_blocks)
        dot = lambda a, b: jnp.dot(a, b, preferred_element_type=jnp.float32)
        return (
            dot(high, right_low[...]) + dot(low, right_high[...]) + dot(high, right_high[...])
        )

    def purify(near, numbers, j):
        gather(near, numbers[0], j)
        mine = jnp.concatenate(
            [near[(own + j) * SLOTS + s] for s in range(SLOTS)], axis=1
        )
        square = product(mine)
        if numbers[1] != numbers[0]:
            gather(near, numbers[1], j)
        return 3.0 * square - 2.0 * product(square)

    def first_step(role):
        j = here[role] - 1
        result = purify(near0, (0, 1), j)
        for u in range(SLOTS):
            near1[(own + j) * SLOTS + u] = result[:, u * block:(u + 1) * block]
        begin(1, role)

    def second_step(role):
        j = here[role] - 1
        result = purify(near1, (2, 2), j)
        for u in range(SLOTS):
            out_ref[j * SLOTS + u] = result[:, u * block:(u + 1) * block]

    inner_arrives(0)
    flip_side(WIDE - 1 - outer_in)
    flip_edge(1)
    flip_edge(2 - 2 * core)
    first_step(1)
    outer_arrives(0)
    flip_side(outer_in)
    flip_edge(2 * core)
    first_step(0)
    relay(1)
    fill(2, 1, 1, False)
    inner_arrives(1)
    second_step(1)
    outer_arrives(1)
    second_step(0)
    all_sent(0)
    all_sent(1)


def on_device(rows, cols, density, pattern, retained):
    block = density.shape[-1]
    vmem = pl.BlockSpec(memory_space=pltpu.VMEM)
    out = pl.pallas_call(
        lambda *refs: kernel(rows, cols, *refs),
        out_shape=jax.ShapeDtypeStruct((SITES * SLOTS, block, block), jnp.float32),
        in_specs=[pl.BlockSpec(memory_space=pltpu.HBM)] * 3,
        out_specs=vmem,
        scratch_shapes=[
            pltpu.VMEM((FLIPPED + WIDE * SLOTS + 2 * WIDE, block, block), jnp.float32),
            pltpu.VMEM((ZERO_BLOCK + 1, block, block), jnp.float32),
            pltpu.VMEM((3 * SLOTS, block, block), jnp.float32),
            pltpu.VMEM((3 * SLOTS, block, block), jnp.float32),
            pltpu.VMEM((2, SITES, SLOTS), jnp.int32),
            pltpu.VMEM((SITES * SLOTS + 1, block, block), jnp.float32),
            pltpu.VMEM((2 * SITES, block, block), jnp.float32),
            pltpu.VMEM((3 * WIDE, 8, 128), jnp.int32),
            pltpu.SMEM((3 * WIDE, 8, 128), jnp.int32),
            pltpu.SMEM((3 * SITES * SLOTS * SLOTS,), jnp.int32),
            pltpu.VMEM((SLOTS * block, SLOTS * block), jnp.bfloat16),
            pltpu.VMEM((SLOTS * block, SLOTS * block), jnp.bfloat16),
            pltpu.SemaphoreType.DMA((22 * CHUNKS,)),
            pltpu.SemaphoreType.DMA((22 * CHUNKS,)),
            pltpu.SemaphoreType.DMA((8,)),
            pltpu.SemaphoreType.DMA((8,)),
            pltpu.SemaphoreType.DMA((5,)),
        ],
        compiler_params=pltpu.CompilerParams(
            collective_id=0, has_side_effects=True, vmem_limit_bytes=63 * 1024 * 1024
        ),
    )(
        pattern.reshape((SITES, SLOTS)),
        retained.reshape((SITES, SLOTS)),
        density.reshape((SITES * SLOTS, block, block)),
    )
    return out.reshape(density.shape)


def solution(mesh):
    rows, cols = mesh.shape["row"], mesh.shape["col"]
    return jax.shard_map(
        lambda *args: on_device(rows, cols, *args),
        mesh=mesh,
        in_specs=(P("row", "col", None, None, None), P("row", "col", None), P("row", "col", None)),
        out_specs=P("row", "col", None, None, None),
        check_vma=False,
    )
```

```python
import jax
import jax.numpy as jnp
from jax import lax
from jax.experimental import pallas as pl
from jax.experimental.pallas import tpu as pltpu
from jax.sharding import PartitionSpec as P

SLOTS = 4
SITES = 2
WIDE = SITES + 2
CHUNKS = 2
ZERO_BLOCK = 3 * WIDE * SLOTS
FLIPPED = ZERO_BLOCK + 1
MESH = pl.DeviceIdType.MESH


def split(x):
    high = x.astype(jnp.bfloat16)
    low = (x - high.astype(jnp.float32)).astype(jnp.bfloat16)
    return high, low


def kernel(
    rows, cols, pattern_ref, retained_ref, density_ref, out_ref,
    near0, near1, far0, far1, own_codes, held, packed, codes, scalars, table, right_high, right_low,
    send_sem, recv_sem, code_send, code_recv, local_sem,
):
    block = out_ref.shape[-1]
    row, col = lax.axis_index("row"), lax.axis_index("col")
    odd, core = lax.rem(row, 2), lax.rem(col, 2)
    pair = row + 1 - 2 * odd
    onward = lax.rem(row + 2 - 4 * odd + rows, rows)
    backward = lax.rem(row - 2 + 4 * odd + rows, rows)
    beside = (lax.rem(col + cols - 1 + 2 * core, cols), lax.rem(col + cols + 1 - 2 * core, cols))
    here, there = (1 + core, 2 - core), (WIDE - 1 - 3 * core, 3 * core)
    outer_in = 3 * core
    paired, handed = 2 - 2 * odd, 2 * odd
    window_rows = (1, paired, handed)
    own = WIDE + 1

    load = pltpu.make_async_copy(
        density_ref, near0.at[pl.ds(own * SLOTS, SITES * SLOTS)], local_sem.at[0]
    )
    load.start()
    load_held = pltpu.make_async_copy(
        density_ref, held.at[pl.ds(0, SITES * SLOTS)], local_sem.at[2]
    )
    load_held.start()
    held[SITES * SLOTS] = jnp.zeros((block, block), jnp.float32)
    load_codes = [
        pltpu.make_async_copy(ref, own_codes.at[k], local_sem.at[3 + k])
        for k, ref in enumerate((pattern_ref, retained_ref))
    ]
    for copy in load_codes:
        copy.start()
    for j in range(SITES):
        codes[own + j] = jnp.zeros(codes.shape[1:], jnp.int32)
    for copy in load_codes:
        copy.wait()
    for j in range(SITES):
        for k in range(2):
            code = own_codes[k, j:j + 1, :]
            third = jnp.where(code >= 6, 2, jnp.where(code >= 3, 1, 0))
            codes[own + j, k:k + 1, 0:SLOTS] = code + 2 * third - 6
            codes[own + j, 2 + k:3 + k, 0:SLOTS] = code + third - 5
    own_scalars = pltpu.make_async_copy(
        codes.at[pl.ds(own, SITES)], scalars.at[pl.ds(own, SITES)], local_sem.at[1]
    )
    own_scalars.start()
    near0[ZERO_BLOCK] = jnp.zeros((block, block), jnp.float32)
    near1[ZERO_BLOCK] = jnp.zeros((block, block), jnp.float32)

    barrier = pltpu.get_barrier_semaphore()
    others = [(pair, col), (onward, col), (backward, col), (row, beside[0]), (row, beside[1])]
    for other in others:
        pl.semaphore_signal(barrier, inc=1, device_id=other, device_id_type=MESH)
    pl.semaphore_wait(barrier, len(others))

    def send(from_ref, ref, source, target, size, sems, index, device):
        return pltpu.make_async_remote_copy(
            src_ref=from_ref.at[pl.ds(source, size)],
            dst_ref=ref.at[pl.ds(target, size)],
            send_sem=sems[0].at[index],
            recv_sem=sems[1].at[index],
            device_id=device,
            device_id_type=MESH,
        )

    def code_copy(index, source, target, size, device):
        return send(codes, codes, source, target, size, (code_send, code_recv), index, device)

    def block_copy(step, kind, chunk, part, source, target, device, from_ref, to_ref, start=None):
        index = (step * 11 + kind) * CHUNKS + chunk
        first = source * SLOTS + chunk * part if start is None else start
        return send(
            from_ref, to_ref, first, target * SLOTS + chunk * part,
            part, (send_sem, recv_sem), index, device,
        )

    parts = (2 // CHUNKS, SLOTS // CHUNKS)
    nears, fars = (near0, near1), (far0, far1)

    def to_pair(step, role, chunk):
        column, part = here[role], parts[step]
        target = handed * WIDE + column
        if step == 0:
            start = (column - 1) * 2 + chunk * part
            return block_copy(0, role, chunk, part, 0, target, (pair, col), packed, near0, start)
        return block_copy(
            1, role, chunk, part, WIDE + column, target, (pair, col), near1, near1
        )

    def hand_on(step, role, chunk):
        near, far = nears[step], fars[step]
        if role == 2:
            return block_copy(
                step, 4, chunk, parts[step], paired, handed, (onward, col), far, far
            )
        column = here[role]
        return block_copy(
            step, 2 + role, chunk, parts[step],
            paired * WIDE + column, handed * WIDE + column, (onward, col), near, near,
        )

    def sideways(step, place, role, chunk):
        part = SLOTS // CHUNKS if place == 0 else parts[step]
        near, far = nears[step], fars[step]
        base = window_rows[place] * WIDE
        target = base + there[1] if role else window_rows[place]
        return block_copy(
            step, 5 + 2 * place + role, chunk, part,
            base + here[role], target, (row, beside[role]), near, near if role else far,
        )

    def begin_row(step, role):
        for chunk in range(CHUNKS):
            sideways(step, 0, role, chunk).start()

    def begin_pair(step, role):
        for chunk in range(CHUNKS):
            to_pair(step, role, chunk).start()

    def relay(step):
        for role in ((0, 1), (1, 0))[step]:
            for chunk in range(CHUNKS):
                to_pair(step, role, chunk).wait_recv()
                hand_on(step, role, chunk).start()
                sideways(step, 1, role, chunk).start()

        def inner():
            for chunk in range(CHUNKS):
                hand_on(step, 1, chunk).wait_recv()
                sideways(step, 2, 1, chunk).start()

        if step == 1:
            inner()
        hand_on(step, 0, 0).wait_recv()
        sideways(step, 2, 0, 0).start()
        sideways(step, 1, 0, 1).wait_recv()
        hand_on(step, 2, 1).start()
        hand_on(step, 0, 1).wait_recv()
        if step == 0:
            inner()

    def inner_arrives(step):
        for chunk in range(CHUNKS):
            for place in range(3):
                sideways(step, place, 1, chunk).wait_recv()

    def outer_arrives(step):
        for chunk in range(CHUNKS):
            sideways(step, 0, 0, chunk).wait_recv()
        sideways(step, 1, 0, 0).wait_recv()
        sideways(step, 2, 0, 0).wait_recv()
        hand_on(step, 2, 1).wait_recv()
        near, far = nears[step], fars[step]
        for window_row in range(3):
            count = SLOTS if step == 1 or window_row == 1 else 2
            for t in range(count):
                near[(window_row * WIDE + outer_in) * SLOTS + t] = far[window_row * SLOTS + t]

    def all_sent(step):
        for chunk in range(CHUNKS):
            for role in range(2):
                to_pair(step, role, chunk).wait_send()
                hand_on(step, role, chunk).wait_send()
                for place in range(3):
                    if (place, role, chunk) != (2, 0, 1):
                        sideways(step, place, role, chunk).wait_send()
        hand_on(step, 2, 1).wait_send()

    def flip(source, target):
        near0[target] = near0[source].T

    codes_pair = code_copy(0, own, handed * WIDE + 1, SITES, (pair, col))
    codes_on = code_copy(1, paired * WIDE + 1, handed * WIDE + 1, SITES, (onward, col))
    codes_side = [
        [
            code_copy(
                2 + 2 * place + role, window_row * WIDE + here[role],
                window_row * WIDE + there[role], 1, (row, beside[role]),
            )
            for role in range(2)
        ]
        for place, window_row in enumerate(window_rows)
    ]
    codes_pair.start()
    for copy in codes_side[0]:
        copy.start()
    load.wait()
    begin_row(0, 0)
    load_held.wait()
    own_scalars.wait()
    for j in range(SITES):
        packed[2 * j] = held[j * SLOTS]
        found = jnp.int32(SITES * SLOTS)
        for t in range(1, SLOTS):
            found = jnp.where(scalars[own + j, 0, t] == 1, j * SLOTS + t, found)
        packed[2 * j + 1] = held[found]
    for role in range(2):
        begin_pair(0, role)
    begin_row(0, 1)
    for j in range(SITES):
        for t in range(1, SLOTS):
            flip((own + j) * SLOTS + t, FLIPPED + (1 + j) * SLOTS + t)
    codes_pair.wait_recv()
    codes_on.start()
    for copy in codes_side[1]:
        copy.start()
    codes_on.wait_recv()
    for copy in codes_side[2]:
        copy.start()
    relay(0)
    for place in range(3):
        for copy in codes_side[place]:
            copy.wait()
    codes_pair.wait_send()
    codes_on.wait_send()
    to_scalars = pltpu.make_async_copy(codes, scalars, local_sem.at[1])
    to_scalars.start()
    to_scalars.wait()

    def fill(number, left_row, right_row, symmetric):
        def one(j, s):
            first = scalars[own + j, left_row, s]
            site = own + j + scalars[own + j, 2 + left_row, s]
            second = [scalars[site, right_row, t] for t in range(SLOTS)]
            in_row = (site >= WIDE) & (site < 2 * WIDE)
            for u in range(SLOTS):
                rest = scalars[own + j, 1, u] - first
                found = jnp.int32(ZERO_BLOCK)
                for t in range(SLOTS):
                    found = jnp.where(second[t] == rest, site * SLOTS + t, found)
                if symmetric:
                    last = own + j + scalars[own + j, 3, u]
                    reverse = jnp.int32(ZERO_BLOCK)
                    for t in range(SLOTS):
                        reverse = jnp.where(
                            scalars[last, right_row, t] == -rest,
                            FLIPPED + (last - WIDE) * SLOTS + t, reverse,
                        )
                    last_in_row = (last >= WIDE) & (last < 2 * WIDE)
                    edge = FLIPPED + WIDE * SLOTS + jnp.where(last < WIDE, last, last - WIDE)
                    sent = jnp.where(
                        rest == 0, site * SLOTS,
                        jnp.where(rest == 1, site * SLOTS + 1, jnp.where(rest == -1, edge, reverse)),
                    )
                    usable = (found != ZERO_BLOCK) & (
                        last_in_row | (rest == 0) | (rest == 1) | (rest == -1)
                    )
                    sent = jnp.where(usable, sent, ZERO_BLOCK)
                    found = jnp.where(in_row, found, sent)
                table[((number * SITES + j) * SLOTS + s) * SLOTS + u] = found

        for j in range(SITES):
            for s in range(SLOTS):
                one(j, s)

    fill(0, 0, 0, True)
    fill(1, 1, 0, True)

    def flip_side(column):
        for t in range(1, SLOTS):
            flip((WIDE + column) * SLOTS + t, FLIPPED + column * SLOTS + t)

    def flip_edge(column):
        for k in range(2):
            flip((2 * k * WIDE + column) * SLOTS + 1, FLIPPED + (SLOTS + k) * WIDE + column)

    def gather(near, number, j, start=0):
        for s in range(start, SLOTS):
            for u in range(SLOTS):
                found = table[((number * SITES + j) * SLOTS + s) * SLOTS + u]
                high, low = split(near[found])
                place = (pl.ds(s * block, block), pl.ds(u * block, block))
                right_high[place] = high
                right_low[place] = low

    def product(left_blocks):
        high, low = split(left_blocks)
        dot = lambda a, b: jnp.dot(a, b, preferred_element_type=jnp.float32)
        return (
            dot(high, right_low[...]) + dot(low, right_high[...]) + dot(high, right_high[...])
        )

    def purify(near, numbers, j):
        gather(near, numbers[0], j)
        mine = jnp.concatenate(
            [near[(own + j) * SLOTS + s] for s in range(SLOTS)], axis=1
        )
        square = product(mine)
        if numbers[1] != numbers[0]:
            gather(near, numbers[1], j, 1)
        return 3.0 * square - 2.0 * product(square)

    def first_step(role):
        j = here[role] - 1
        result = purify(near0, (0, 1), j)
        for u in range(SLOTS):
            near1[(own + j) * SLOTS + u] = result[:, u * block:(u + 1) * block]
        begin_row(1, role)
        begin_pair(1, role)

    def second_step(role):
        j = here[role] - 1
        result = purify(near1, (2, 2), j)
        for u in range(SLOTS):
            out_ref[j * SLOTS + u] = result[:, u * block:(u + 1) * block]

    inner_arrives(0)
    flip_side(WIDE - 1 - outer_in)
    flip_edge(1)
    flip_edge(2 - 2 * core)
    first_step(1)
    outer_arrives(0)
    flip_side(outer_in)
    flip_edge(2 * core)
    first_step(0)
    relay(1)
    fill(2, 1, 1, False)
    inner_arrives(1)
    second_step(1)
    outer_arrives(1)
    second_step(0)
    all_sent(0)
    all_sent(1)


def on_device(rows, cols, density, pattern, retained):
    block = density.shape[-1]
    vmem = pl.BlockSpec(memory_space=pltpu.VMEM)
    out = pl.pallas_call(
        lambda *refs: kernel(rows, cols, *refs),
        out_shape=jax.ShapeDtypeStruct((SITES * SLOTS, block, block), jnp.float32),
        in_specs=[pl.BlockSpec(memory_space=pltpu.HBM)] * 3,
        out_specs=vmem,
        scratch_shapes=[
            pltpu.VMEM((FLIPPED + WIDE * SLOTS + 2 * WIDE, block, block), jnp.float32),
            pltpu.VMEM((ZERO_BLOCK + 1, block, block), jnp.float32),
            pltpu.VMEM((3 * SLOTS, block, block), jnp.float32),
            pltpu.VMEM((3 * SLOTS, block, block), jnp.float32),
            pltpu.VMEM((2, SITES, SLOTS), jnp.int32),
            pltpu.VMEM((SITES * SLOTS + 1, block, block), jnp.float32),
            pltpu.VMEM((2 * SITES, block, block), jnp.float32),
            pltpu.VMEM((3 * WIDE, 8, 128), jnp.int32),
            pltpu.SMEM((3 * WIDE, 8, 128), jnp.int32),
            pltpu.SMEM((3 * SITES * SLOTS * SLOTS,), jnp.int32),
            pltpu.VMEM((SLOTS * block, SLOTS * block), jnp.bfloat16),
            pltpu.VMEM((SLOTS * block, SLOTS * block), jnp.bfloat16),
            pltpu.SemaphoreType.DMA((22 * CHUNKS,)),
            pltpu.SemaphoreType.DMA((22 * CHUNKS,)),
            pltpu.SemaphoreType.DMA((8,)),
            pltpu.SemaphoreType.DMA((8,)),
            pltpu.SemaphoreType.DMA((5,)),
        ],
        compiler_params=pltpu.CompilerParams(
            collective_id=0, has_side_effects=True, vmem_limit_bytes=32 * 1024 * 1024
        ),
    )(
        pattern.reshape((SITES, SLOTS)),
        retained.reshape((SITES, SLOTS)),
        density.reshape((SITES * SLOTS, block, block)),
    )
    return out.reshape(density.shape)


def solution(mesh):
    rows, cols = mesh.shape["row"], mesh.shape["col"]
    return jax.shard_map(
        lambda *args: on_device(rows, cols, *args),
        mesh=mesh,
        in_specs=(P("row", "col", None, None, None), P("row", "col", None), P("row", "col", None)),
        out_specs=P("row", "col", None, None, None),
        check_vma=False,
    )
```
